256 devices in a mesh: redist: 32 (over z, x_lo, core), summa: 8 (over y, x_hi).
Axes of the slice: x: 4 (x_hi: 2, x_lo: 2; x = x_hi * 2 + x_lo), y: 4, z: 8, core: 2. Of those that a mesh axis runs over, the one named last changes fastest.
Arguments:
- amplitudes: float32 [1024, 22528], P('summa', 'redist'), may hold values from -6 to 6
- integrals: float32 [22528, 22528], P('redist', 'summa'), may hold values from -0.0390625 to 0.0390625
Outputs:
- ladder: float32 [1024, 22528], P('redist', 'summa')
The draws below stay inside these ranges and needn't reach their ends.
All inputs are finite; a program needn't handle non-finite values.
Results may differ from the reference program's by a relative error of at most 0.000075.
Values sent between devices are 32-bit elements; how exact they have to be, the bound alone decides.
No kernel may reach another device: no remote copies, remote signals or barrier semaphores. Data moves between devices by JAX's collectives and lax.ppermute only.
A program may use at most 64 MiB of HBM per device.

```python
import jax
import jax.numpy as jnp
from jax import lax

PAIRS = 1024
K = 22528
M = 22528


def strengthened(array, stream_key, source, target, shards_of, factor):
    def block_of(dim):
        return (jnp.arange(array.shape[dim]) // (array.shape[dim] // shards_of)).reshape((-1,) + (1,) * (array.ndim - 1 - dim))

    near = jax.random.permutation(stream_key, shards_of)[block_of(target)]
    second = (block_of(target) + shards_of // 2) % shards_of
    return jnp.where((block_of(source) == near) | (block_of(source) == second), factor * array, array)


def block_levels(own_key, shape, shards, low, top_value):
    level, own = 1.0, jax.random.fold_in(own_key, 6)
    for axis_at, blocks in shards:
        steps = jnp.exp(jax.random.uniform(jax.random.fold_in(own, axis_at), (blocks,), jnp.float32, low / len(shards), top_value / len(shards)))
        level = level * jnp.repeat(steps, shape[axis_at] // blocks).reshape([-1 if axis == axis_at else 1 for axis in range(len(shape))])
    return level


def normal_values(key, dims, width, limit, shards=(), dtype=jnp.bfloat16):
    array = jax.random.normal(key, dims, jnp.float32) * width
    if len(shards) > 0:
        array = block_levels(key, dims, shards, -0.22, 0.18) * array
    return jnp.clip(array, min=-limit, max=limit).astype(dtype)


def heavy_noise(own_key, extent, width, reach, split, heavy, dtype=jnp.bfloat16):
    values = width * jax.random.normal(own_key, extent, jnp.float32)
    if split:
        values = values * block_levels(own_key, extent, split, -0.22, 0.18)
    return jnp.clip(strengthened(values, jax.random.fold_in(own_key, 3), *heavy), -reach, reach).astype(dtype)


def setup_inputs(seed: int = 0) -> dict:
    key_of = jax.random.split(jax.random.key(seed), 3)
    amplitudes = heavy_noise(key_of[0], (PAIRS, K), 1.0, 6.0, ((0, 8), (1, 32)), (1, 0, 32, 2.75), jnp.float32)
    integrals = normal_values(key_of[1], (K, M), K ** -0.5, 0.0390625, ((0, 32), (1, 8)), jnp.float32)
    return {"amplitudes": amplitudes, "integrals": integrals}


def reference(amplitudes, integrals):
    products = jnp.dot(amplitudes, integrals, precision=lax.Precision.HIGHEST, preferred_element_type=jnp.float32)
    return 0.5 * products
```

```python
import jax
import jax.numpy as jnp
from jax import lax
from jax.sharding import Mesh, PartitionSpec as P

X_FIRST = 12


def shift(x, axis, by):
    n = lax.axis_size(axis)
    return lax.ppermute(x, axis, [(i, (i + by) % n) for i in range(n)])


def gather_panels(own):
    with jax.named_scope("gather_rows"):
        half = own.shape[0] // 2
        rows = [own, shift(own, "xh", 1)]
        out = [rows]
        up = [shift(r, "y", 1) for r in rows]
        down = [shift(r, "y", -1) for r in rows]
        far = [
            jnp.concatenate([shift(u[:half], "y", 1), shift(d[half:], "y", -1)], 0)
            for u, d in zip(up, down)
        ]
        return [rows, down, far, up]


def ring(part, sign):
    a = part(4 * sign)
    for k in (3, 2, 1):
        a = shift(a, "z", sign) + part(k * sign)
    a = shift(a, "z", sign)
    b = part(-3 * sign)
    for k in (2, 1):
        b = shift(b, "z", -sign) + part(-k * sign)
    b = shift(b, "z", -sign)
    return part(0) + a + b


def dot(a, b):
    return jnp.dot(a, b, precision=lax.Precision.HIGH, preferred_element_type=jnp.float32)


def per_device(amplitudes, integrals):
    z, xl, c = (lax.axis_index(n) for n in ("z", "xl", "c"))
    y, xh = lax.axis_index("y"), lax.axis_index("xh")
    depth, width = integrals.shape
    own = amplitudes.reshape(2, 2, 32, depth)
    own = jnp.where(xl == 1, own[::-1], own)
    own = jnp.where(c == 1, own[:, ::-1], own)
    own = own.transpose(1, 0, 2, 3).reshape(128, depth)
    panels = gather_panels(own)

    rows = jnp.zeros((2, 8, 64, depth), jnp.float32)
    for yr in range(4):
        for xr in range(2):
            owner = ((y + yr) & 3) * 2 + ((xh + xr) & 1)
            panel = panels[yr][xr].reshape(2, 1, 64, depth)
            rows = lax.dynamic_update_slice(rows, panel, (0, (owner - z) & 7, 0, 0))
    keep_rows = rows[0].reshape(512, depth)
    send_rows = rows[1].reshape(512, depth)

    cut = width - X_FIRST * 128

    def core_sum(cols):
        b = integrals[:, cols]
        w = b.shape[1]
        with jax.named_scope("send_half"):
            got = shift(dot(send_rows, b), "c", 1).reshape(8, 2, 32, w)
        with jax.named_scope("keep_half"):
            kept = dot(keep_rows, b).reshape(8, 2, 32, w)
        return kept, got

    kept, got = core_sum(slice(0, cut))
    with jax.named_scope("z_first"):
        far = ring(lambda k: kept[k % 8, 1] + got[k % 8, 1], 1)
        near = ring(lambda k: kept[k % 8, 0] + got[k % 8, 0], -1)
        left = near + shift(far, "xl", 1)

    kept2, got2 = core_sum(slice(cut, width))
    with jax.named_scope("x_first"):
        other = shift(kept2[:, 1] + got2[:, 1], "xl", 1)

        def part(lo):
            return lambda k: (
                kept2[k % 8, 0, lo : lo + 16] + got2[k % 8, 0, lo : lo + 16] + other[k % 8, lo : lo + 16]
            )

        right = jnp.concatenate([ring(part(0), 1), ring(part(16), -1)], 0)
    return 0.5 * jnp.concatenate([left, right], 1)


def solution(mesh):
    fine = Mesh(mesh.devices.reshape(8, 2, 2, 4, 2), ("z", "xl", "c", "y", "xh"))
    redist, summa = ("z", "xl", "c"), ("y", "xh")
    return jax.shard_map(
        per_device,
        mesh=fine,
        in_specs=(P(summa, redist), P(redist, summa)),
        out_specs=P(redist, summa),
        check_vma=False,
    )
```

```python
import functools

import jax
import jax.numpy as jnp
from jax import lax
from jax.experimental import pallas as pl
from jax.experimental.pallas import tpu as pltpu
from jax.sharding import Mesh, PartitionSpec as P

X_FIRST = 10
TILE = 256

SLOTS = 0x63745210

VMEM = pl.BlockSpec(memory_space=pltpu.VMEM)
SMEM = pl.BlockSpec(memory_space=pltpu.SMEM)
ANY = pl.BlockSpec(memory_space=pl.ANY)
HBM = pl.BlockSpec(memory_space=pltpu.HBM)

HEAVY, LIGHT = 20_000_000_000, 1


def shift(x, axis, by):
    n = lax.axis_size(axis)
    return lax.ppermute(x, axis, [(i, (i + by) % n) for i in range(n)])


def local(body, ins, deps, outs, scratch=(), scalars=(), through=(), pinned=True, big=(), weight=HEAVY):
    pin = lambda x: pltpu.with_memory_space_constraint(x, pltpu.VMEM)
    sizes = [len(scalars), len(ins), len(big), len(through), len(deps), len(outs), len(through), len(scratch)]

    def kernel(*refs):
        groups, at = [], 0
        for n in sizes:
            groups.append(refs[at : at + n])
            at += n
        s, i, g, _, _, o, _, t = groups
        body(*([s[0]] if s else []), [*i, *g], o, *([t] if t else []))

    kind = pltpu.VMEM if pinned else jax.ShapeDtypeStruct
    first = len(scalars) + len(ins) + len(big)
    return pl.pallas_call(
        kernel,
        in_specs=[SMEM] * len(scalars) + [VMEM] * len(ins) + [HBM] * len(big) + [VMEM] * len(through) + [ANY] * len(deps),
        out_specs=[VMEM] * (len(outs) + len(through)),
        out_shape=[kind(s, d) for s, d in outs] + [pltpu.VMEM(x.shape, x.dtype) for x in through],
        input_output_aliases={first + i: len(outs) + i for i in range(len(through))},
        scratch_shapes=list(scratch),
        compiler_params=pltpu.CompilerParams(vmem_limit_bytes=8 * 1024 * 1024),
        cost_estimate=pl.CostEstimate(flops=weight, bytes_accessed=1, transcendentals=0),
    )(*scalars, *map(pin, ins), *(pltpu.with_memory_space_constraint(x, pltpu.HBM) for x in big), *map(pin, through), *deps)


def split(x):
    high = x.astype(jnp.bfloat16)
    return high, (x - high.astype(jnp.float32)).astype(jnp.bfloat16)


def rows_in(row_refs, places, a_high, a_low):
    for ref, row, half, slot in places:
        to = half * 256 + slot * 64
        a_high[to : to + 64], a_low[to : to + 64] = split(row_refs[ref][row : row + 64])


def multiply(a_high, a_low, high, low, keep_ref, send_ref, cols):
    mul = functools.partial(jnp.dot, preferred_element_type=jnp.float32)
    sums = mul(a_high[...], high) + (mul(a_low[...], high) + mul(a_high[...], low))
    keep_ref[:, cols] = sums[:256]
    send_ref[:, cols] = sums[256:]


def tile(i):
    return pl.ds(pl.multiple_of(i * TILE, TILE), TILE)


def early_products(panels, places, b, first, tiles, deps, through=(), weight=HEAVY):
    depth = b.shape[0]

    def body(ins, outs, scratch):
        *row_refs, b_ref = ins
        keep_ref, send_ref, high_ref, low_ref = outs
        a_high, a_low, held, sems = scratch

        def fetch(i):
            return pltpu.make_async_copy(b_ref.at[:, tile(first + i)], held.at[i & 1], sems.at[i & 1])

        fetch(0).start()
        rows_in(row_refs, places, a_high, a_low)

        @pl.loop(0, tiles)
        def _(i):
            @pl.when(i + 1 < tiles)
            def _():
                fetch(i + 1).start()

            fetch(i).wait()
            high, low = split(held[i & 1])
            high_ref[:, tile(i)], low_ref[:, tile(i)] = high, low
            multiply(a_high, a_low, high, low, keep_ref, send_ref, tile(i))

    width = tiles * TILE
    outs = [((256, width), jnp.float32)] * 2 + [((depth, width), jnp.bfloat16)] * 2
    scratch = [pltpu.VMEM((512, depth), jnp.bfloat16)] * 2
    scratch += [pltpu.VMEM((2, depth, TILE), jnp.float32), pltpu.SemaphoreType.DMA((2,))]
    return local(body, panels, deps, outs, scratch, through=through, big=[b], weight=weight)


def late_products(panels, places, high, low, deps):
    depth, width = high.shape

    def body(ins, outs, scratch):
        *row_refs, high_ref, low_ref = ins
        a_high, a_low = scratch
        rows_in(row_refs, places, a_high, a_low)

        @pl.loop(0, width // TILE)
        def _(i):
            multiply(a_high, a_low, high_ref[:, tile(i)], low_ref[:, tile(i)], *outs, tile(i))

    outs = [((256, width), jnp.float32)] * 2
    return local(body, [*panels, high, low], deps, outs, [pltpu.VMEM((512, depth), jnp.bfloat16)] * 2)


def late_halves(up, down, deps):
    def body(ins, outs):
        outs[0][...] = ins[0][:64]
        outs[1][...] = ins[1][64:128]

    return local(body, [up, down], deps, [((64, up.shape[1]), jnp.float32)] * 2)


def x_part(kept, got, deps):
    def body(ins, outs):
        for i in range(4):
            rows = slice(64 * i + 32, 64 * i + 64)
            outs[0][32 * i : 32 * i + 32] = ins[0][rows] + ins[1][rows]

    return local(body, [kept, got], deps, [((128, kept.shape[1]), jnp.float32)])[0]


class Ring:
    def __init__(self, slots, lots, n):
        self.slots, self.lots, self.n = slots, lots, n
        self.i = 4
        self.width = lots[0][0].shape[1]

    def kernel(self, ins, moves, outs, deps):
        n, count, sources = self.n, len(ins), [*self.lots[0], *self.lots[1]]
        strides = [v.shape[0] // 4 for v in self.lots[0]]

        def body(slots, refs, out_refs):
            lots = refs[count : count + len(strides)], refs[count + len(strides) :]
            for out, at, k, low, adds in moves:
                s = slots[k % 8]

                def write(lot, s):
                    total = sum(
                        ref[pl.ds(pl.multiple_of(s * stride + low, n), n)] for ref, stride in zip(lot, strides)
                    )
                    for source, row in adds:
                        total = total + refs[source][row : row + n]
                    out_refs[out][at : at + n] = total

                pl.when(s < 4)(functools.partial(write, lots[0], s))
                pl.when(s >= 4)(functools.partial(write, lots[1], s - 4))

        shapes = [((rows, self.width), jnp.float32) for rows in outs]
        return local(body, [*ins, *sources], deps, shapes, scalars=[self.slots])

    def begin(self, deps):
        n = self.n
        moves = [(0, 0, 4, 0, ()), (0, n, 3, n, ()), (1, 0, -4, n, ()), (1, n, -3, 0, ())]
        self.sends = self.kernel([], moves, [2 * n, 2 * n], deps)

    def hop(self):
        self.got = [shift(self.sends[0], "z", 1), shift(self.sends[1], "z", -1)]

    def add(self, deps):
        n = self.n
        self.i -= 1
        i = self.i
        if i > 1:
            moves = [
                (0, 0, i, 0, [(0, 0)]),
                (0, n, i - 1, n, [(0, n)]),
                (1, 0, -i, n, [(1, 0)]),
                (1, n, 1 - i, 0, [(1, n)]),
            ]
            self.sends = self.kernel(self.got, moves, [2 * n, 2 * n], deps)
        elif i == 1:
            self.rest = self.got
            moves = [(0, 0, 1, 0, [(0, 0)]), (1, 0, -1, n, [(1, 0)])]
            self.sends = self.kernel(self.got, moves, [n, n], deps)
        else:
            moves = [(0, 0, 0, 0, [(0, 0), (3, n)]), (1, 0, 0, n, [(1, 0), (2, n)])]
            return self.kernel([*self.got, *self.rest], moves, [n, n], deps)


def finish(left, from_x, right_a, right_b):
    cut = left.shape[1]

    def body(ins, outs):
        out = outs[0]
        out[:, :cut] = 0.5 * (ins[0][...] + ins[1][...])
        out[:16, cut:] = 0.5 * ins[2][...]
        out[16:, cut:] = 0.5 * ins[3][...]

    shape = (32, cut + right_a.shape[1])
    return local(body, [left, from_x, right_a, right_b], [], [(shape, jnp.float32)], pinned=False)[0]


def per_device(amplitudes, integrals):
    z, xl, c = (lax.axis_index(n) for n in ("z", "xl", "c"))
    y, xh = lax.axis_index("y"), lax.axis_index("xh")
    depth, width = integrals.shape
    x_tiles = X_FIRST * 128 // TILE
    z_tiles = width // TILE - x_tiles

    owner = (z + jnp.arange(8, dtype=jnp.int32)) & 7
    code = (((owner >> 1) - y) & 3) * 2 + ((owner ^ xh) & 1)
    slots = (SLOTS >> (code * 4)) & 7

    own = amplitudes.reshape(2, 2, 32, depth)
    own = jnp.where(xl == 1, own[::-1], own)
    own = jnp.where(c == 1, own[:, ::-1], own)
    own = own.transpose(1, 0, 2, 3).reshape(128, depth)

    up, down, other = shift(own, "y", 1), shift(own, "y", -1), shift(own, "xh", 1)
    up2 = shift(jnp.concatenate([other, up[:64]], 0), "y", 1)
    down2 = shift(jnp.concatenate([other, down[64:]], 0), "y", -1)

    early = [own, other, down, up]
    early_places = [(i, 64 * half, half, i) for i in range(4) for half in range(2)]
    late_places = [(0, 128, 0, 0), (1, 128, 1, 0), (2, 0, 0, 3), (3, 0, 1, 3)]
    late_places += [(ref, 64 * half, half, slot) for slot, ref in ((1, 1), (2, 0)) for half in range(2)]

    kept_x0, sent_x0, *b_x = early_products(early, early_places, integrals, z_tiles, x_tiles, [])
    kept_z0, sent_z0, *b_z, sent_x0 = early_products(
        early, early_places, integrals, 0, z_tiles, [kept_x0], [sent_x0], LIGHT
    )
    got_x0, got_z0 = shift(sent_x0, "c", 1), shift(sent_z0, "c", 1)
    far_up, far_down = late_halves(up2, down2, [kept_z0])
    late = [up2, down2, shift(far_up, "y", 1), shift(far_down, "y", -1)]
    x_send0 = x_part(kept_x0, got_x0, [far_up])
    other0 = shift(x_send0, "xl", 1)

    kept_z1, sent_z1 = late_products(late, late_places, *b_z, [x_send0])
    got_z1 = shift(sent_z1, "c", 1)
    kept_x1, sent_x1 = late_products(late, late_places, *b_x, [kept_z1])
    got_x1 = shift(sent_x1, "c", 1)

    first = Ring(slots, ([kept_z0, got_z0], [kept_z1, got_z1]), 32)
    first.begin([kept_x1])
    first.hop()
    x_send1 = x_part(kept_x1, got_x1, [*first.sends, other0])
    other1 = shift(x_send1, "xl", 1)
    first.add([x_send1])
    first.hop()
    second = Ring(slots, ([kept_x0, got_x0, other0], [kept_x1, got_x1, other1]), 16)
    second.begin(first.sends)
    for _ in range(2):
        second.hop()
        first.add(second.sends)
        first.hop()
        second.add(first.sends)
    second.hop()
    near, far_sum = first.add(second.sends)
    from_x = shift(far_sum, "xl", 1)
    second.add([far_sum])
    second.hop()
    right = second.add([])
    return finish(near, from_x, *right)


def solution(mesh):
    fine = Mesh(mesh.devices.reshape(8, 2, 2, 4, 2), ("z", "xl", "c", "y", "xh"))
    redist, summa = ("z", "xl", "c"), ("y", "xh")
    return jax.shard_map(
        per_device,
        mesh=fine,
        in_specs=(P(summa, redist), P(redist, summa)),
        out_specs=P(redist, summa),
        check_vma=False,
    )
```

```python
import functools

import jax
import jax.numpy as jnp
from jax import lax
from jax.experimental import pallas as pl
from jax.experimental.pallas import tpu as pltpu
from jax.sharding import Mesh, PartitionSpec as P

X_FIRST = 10
TILE = 256

SLOTS = 0x63745210

VMEM = pl.BlockSpec(memory_space=pltpu.VMEM)
SMEM = pl.BlockSpec(memory_space=pltpu.SMEM)
ANY = pl.BlockSpec(memory_space=pl.ANY)
HBM = pl.BlockSpec(memory_space=pltpu.HBM)

HEAVY, LIGHT = 20_000_000_000, 1


def shift(x, axis, by):
    n = lax.axis_size(axis)
    return lax.ppermute(x, axis, [(i, (i + by) % n) for i in range(n)])


def local(body, ins, deps, outs, scratch=(), scalars=(), through=(), pinned=True, big=(), weight=HEAVY, limit=4):
    pin = lambda x: pltpu.with_memory_space_constraint(x, pltpu.VMEM)
    sizes = [len(scalars), len(ins), len(big), len(through), len(deps), len(outs), len(through), len(scratch)]

    def kernel(*refs):
        groups, at = [], 0
        for n in sizes:
            groups.append(refs[at : at + n])
            at += n
        s, i, g, _, _, o, through_outs, t = groups
        body(*([s[0]] if s else []), [*i, *g], [*o, *through_outs], *([t] if t else []))

    kind = pltpu.VMEM if pinned else jax.ShapeDtypeStruct
    first = len(scalars) + len(ins) + len(big)
    return pl.pallas_call(
        kernel,
        in_specs=[SMEM] * len(scalars) + [VMEM] * len(ins) + [HBM] * len(big) + [VMEM] * len(through) + [ANY] * len(deps),
        out_specs=[VMEM] * (len(outs) + len(through)),
        out_shape=[kind(s, d) for s, d in outs] + [pltpu.VMEM(x.shape, x.dtype) for x in through],
        input_output_aliases={first + i: len(outs) + i for i in range(len(through))},
        scratch_shapes=list(scratch),
        compiler_params=pltpu.CompilerParams(vmem_limit_bytes=limit * 1024 * 1024),
        cost_estimate=pl.CostEstimate(flops=weight, bytes_accessed=1, transcendentals=0),
    )(*scalars, *map(pin, ins), *(pltpu.with_memory_space_constraint(x, pltpu.HBM) for x in big), *map(pin, through), *deps)


def split(x):
    high = x.astype(jnp.bfloat16)
    return high, (x - high.astype(jnp.float32)).astype(jnp.bfloat16)


def split_columns(b, sets, deps):
    depth, tiles = b.shape[0], b.shape[1] // TILE

    def body(ins, outs, scratch):
        held, sems = scratch
        copies = [
            pltpu.make_async_copy(ins[0].at[:, i * TILE : (i + 1) * TILE], held.at[i], sems.at[i]) for i in range(tiles)
        ]
        for copy in copies:
            copy.start()
        for j, (first, count) in enumerate(sets):
            for i in range(count):
                copies[first + i].wait()
                cols = slice(i * TILE, (i + 1) * TILE)
                outs[2 * j][:, cols], outs[2 * j + 1][:, cols] = split(held[first + i])

    outs = [((depth, count * TILE), jnp.bfloat16) for _, count in sets for _ in range(2)]
    scratch = [pltpu.VMEM((tiles, depth, TILE), jnp.float32), pltpu.SemaphoreType.DMA((tiles,))]
    parts = local(body, [], deps, outs, scratch, big=[b], limit=12)
    return [parts[i : i + 2] for i in range(0, len(parts), 2)]


def products(panels, places, parts, deps, slots, into=(), joined=False, weight=HEAVY):
    count, depth = len(panels), parts[0][0].shape[0]
    mine = sorted({slot for *_, slot in places})
    first_slot, rows = mine[0], len(mine) * 64
    widths = [high.shape[1] for high, _ in parts]

    def body(ins, outs, scratch):
        a_high, a_low = scratch
        for ref, row, half, slot in places:
            to = half * rows + (slot - first_slot) * 64
            a_high[to : to + 64], a_low[to : to + 64] = split(ins[ref][row : row + 64])
        mul = functools.partial(jnp.dot, preferred_element_type=jnp.float32)
        block = slice(first_slot * 64, first_slot * 64 + rows)
        for j, width in enumerate(widths):
            high_ref, low_ref = ins[count + 2 * j : count + 2 * j + 2]
            keep_ref, send_ref = outs if joined else outs[2 * j : 2 * j + 2]
            first = sum(widths[:j]) if joined else 0
            for i in range(0, width, TILE):
                high, low = high_ref[:, i : i + TILE], low_ref[:, i : i + TILE]
                sums = mul(a_high[...], high) + (mul(a_low[...], high) + mul(a_high[...], low))
                keep_ref[block, first + i : first + i + TILE] = sums[:rows]
                send_ref[block, first + i : first + i + TILE] = sums[rows:]

    out_widths = [sum(widths)] if joined else widths
    outs = [] if into else [((slots * 64, width), jnp.float32) for width in out_widths for _ in range(2)]
    scratch = [pltpu.VMEM((2 * rows, depth), jnp.bfloat16)] * 2
    flat = [p for pair in parts for p in pair]
    return local(body, [*panels, *flat], deps, outs, scratch, through=into, weight=weight, limit=8)


def pack(up, down, other, deps):
    def body(ins, outs):
        up_ref, down_ref, other_ref = ins
        outs[0][:64], outs[0][64:] = other_ref[:64], up_ref[:64]
        outs[1][:64], outs[1][64:] = other_ref[64:], down_ref[64:]
        outs[2][:64], outs[2][64:] = up_ref[64:], down_ref[:64]

    return local(body, [up, down, other], deps, [(up.shape, jnp.float32)] * 3)


def late_halves(up, down, deps):
    def body(ins, outs):
        outs[0][...] = ins[0][:64]
        outs[1][...] = ins[1][:64]

    return local(body, [up, down], deps, [((64, up.shape[1]), jnp.float32)] * 2)


def x_part(lots, width, deps):
    def body(ins, outs):
        at = 0
        for kept, got, (_, _, col) in zip(ins[::2], ins[1::2], lots):
            for i in range(kept.shape[0] // 64):
                block = slice(64 * i + 32, 64 * i + 64), slice(col, col + width)
                outs[0][at : at + 32] = kept[block] + got[block]
                at += 32

    rows = sum(kept.shape[0] for kept, _, _ in lots) // 2
    return local(body, [v for lot in lots for v in lot[:2]], deps, [((rows, width), jnp.float32)], weight=LIGHT)[0]


def gate(deps):
    def body(ins, outs):
        outs[0][...] = jnp.zeros_like(outs[0])

    return local(body, [], deps, [((8, 128), jnp.float32)])


class Ring:
    def __init__(self, slots, lots, n, width):
        self.slots, self.lots, self.n, self.width = slots, lots, n, width
        self.i = 0

    def blocks(self, moves, outs, deps):
        n, width, arrays = self.n, self.width, []
        for _, lot in self.lots:
            arrays += [v for v, *_ in lot if not any(v is w for w in arrays)]
        where = lambda v: next(i for i, w in enumerate(arrays) if w is v)

        def body(slots, refs, out_refs):
            for out, at, k, low in moves:
                s = slots[k % 8]

                def write(first, lot):
                    total = 0.0
                    for v, stride, row, col in lot:
                        rows = pl.ds(pl.multiple_of((s - first) * stride + (row + low), n), n)
                        total = total + refs[where(v)][rows, col : col + width]
                    out_refs[out][at : at + n] = total

                for (first, end), lot in self.lots:
                    pl.when((s >= first) & (s < end))(functools.partial(write, first, lot))

        shapes = [((rows, width), jnp.float32) for rows in outs]
        return local(body, arrays, deps, shapes, scalars=[self.slots])

    def begin(self, deps):
        n = self.n
        moves = [(0, 0, 4, 0), (0, n, 3, n), (1, 0, -4, n), (1, n, -3, 0)]
        self.sends = self.blocks(moves, [2 * n, 2 * n], deps)

    def rest(self):
        n = self.n
        moves, rows = [], []
        for i in (3, 2, 1, 0):
            at = len(rows)
            moves += [(at, 0, i, 0), (at + 1, 0, -i, n)]
            if i > 1:
                moves += [(at, n, i - 1, n), (at + 1, n, 1 - i, 0)]
            rows += [2 * n if i > 1 else n] * 2
        self.addends = self.blocks(moves, rows, self.sends)

    def hop(self):
        self.got = [shift(self.sends[0], "z", 1), shift(self.sends[1], "z", -1)]

    def add(self, deps):
        n, width = self.n, self.width
        up, down = self.addends[2 * self.i : 2 * self.i + 2]
        self.i += 1
        last = self.i == 4
        rows = up.shape[0]

        def body(ins, outs):
            for j in range(2):
                total = ins[j][:rows] + ins[2 + j][...]
                if last:
                    total = total + ins[5 - j][n:]
                outs[j][...] = total

        ins = [*self.got, up, down, *(self.before if last else [])]
        self.before = self.got
        self.sends = local(body, ins, deps, [((rows, width), jnp.float32)] * 2)
        return self.sends


def finish(left, from_x, right_a, right_b):
    cut = left.shape[1]

    def body(ins, outs):
        out = outs[0]
        out[:, :cut] = 0.5 * (ins[0][...] + ins[1][...])
        out[:16, cut:] = 0.5 * ins[2][...]
        out[16:, cut:] = 0.5 * ins[3][...]

    shape = (32, cut + right_a.shape[1])
    return local(body, [left, from_x, right_a, right_b], [], [(shape, jnp.float32)], pinned=False)[0]


def per_device(amplitudes, integrals):
    z, xl, c = (lax.axis_index(n) for n in ("z", "xl", "c"))
    y, xh = lax.axis_index("y"), lax.axis_index("xh")
    depth, width = integrals.shape
    x_tiles = X_FIRST * 128 // TILE
    z_tiles = width // TILE - x_tiles

    owner = (z + jnp.arange(8, dtype=jnp.int32)) & 7
    code = (((owner >> 1) - y) & 3) * 2 + ((owner ^ xh) & 1)
    slots = (SLOTS >> (code * 4)) & 7

    own = amplitudes.reshape(2, 2, 32, depth)
    own = jnp.where(xl == 1, own[::-1], own)
    own = jnp.where(c == 1, own[:, ::-1], own)
    own = own.transpose(1, 0, 2, 3).reshape(128, depth)

    up, down, other = shift(own, "y", 1), shift(own, "y", -1), shift(own, "xh", 1)
    cut, x_width = z_tiles * TILE, x_tiles * TILE
    b_z, b_x = split_columns(integrals, ((0, z_tiles), (z_tiles, x_tiles)), [slots])
    both_halves = lambda ref, slot: [(ref, 64 * half, half, slot) for half in range(2)]
    own_blocks = products([own], both_halves(0, 0), [b_x, b_z], [], 4)
    packed_up, packed_down, packed_x = pack(up, down, other, [own_blocks[0]])
    up2, down2, other2 = shift(packed_up, "y", 1), shift(packed_down, "y", -1), shift(packed_x, "xh", 1)

    early_places = both_halves(0, 1) + both_halves(1, 2) + both_halves(2, 3)
    kept_x0, sent_x0, kept_z0, sent_z0 = products(
        [other, down, up], early_places, [b_x, b_z], [], 4, own_blocks, weight=LIGHT
    )
    got_x0, got_z0 = shift(sent_x0, "c", 1), shift(sent_z0, "c", 1)

    far_up, far_down = late_halves(up2, down2, [kept_z0, other2])
    other_far = [shift(far_up, "y", 1), shift(far_down, "y", -1)]
    x_send0 = x_part([(kept_x0, got_x0, 0)], x_width, [far_up])
    other0 = shift(x_send0, "xl", 1)

    late_places = [(0, 64, 0, 0), (1, 64, 1, 0), (2, 64, 0, 1), (1, 0, 1, 1), (0, 0, 0, 2), (2, 0, 1, 2)]
    kept1, sent1 = products([up2, down2, other2], late_places, [b_z, b_x], [x_send0], 3, joined=True)
    got1 = shift(sent1, "c", 1)
    kept_z2, sent_z2, kept_x2, sent_x2 = products(
        other_far, [(0, 0, 0, 0), (1, 0, 1, 0)], [b_z, b_x], [kept1, got_z0], 1
    )
    got_z2, got_x2 = shift(sent_z2, "c", 1), shift(sent_x2, "c", 1)

    z_lots = [
        ((0, 4), [(kept_z0, 64, 0, 0), (got_z0, 64, 0, 0)]),
        ((4, 7), [(kept1, 64, 0, 0), (got1, 64, 0, 0)]),
        ((7, 8), [(kept_z2, 64, 0, 0), (got_z2, 64, 0, 0)]),
    ]
    first = Ring(slots, z_lots, 32, cut)
    first.begin(gate([kept_z2]))
    first.hop()
    first.rest()
    x_send1 = x_part([(kept1, got1, cut), (kept_x2, got_x2, 0)], x_width, [first.addends[0], other0])
    other1 = shift(x_send1, "xl", 1)
    first.add([x_send1])
    first.hop()
    x_lots = [
        ((0, 4), [(kept_x0, 64, 0, 0), (got_x0, 64, 0, 0), (other0, 32, 0, 0)]),
        ((4, 7), [(kept1, 64, 0, cut), (got1, 64, 0, cut), (other1, 32, 0, 0)]),
        ((7, 8), [(kept_x2, 64, 0, 0), (got_x2, 64, 0, 0), (other1, 32, 96, 0)]),
    ]
    second = Ring(slots, x_lots, 16, x_width)
    second.begin(first.sends)
    second.hop()
    second.rest()
    first.add([second.addends[0]])
    first.hop()
    second.add(first.sends)
    second.hop()
    first.add(second.sends)
    first.hop()
    second.add(first.sends)
    second.hop()
    near, far_sum = first.add(second.sends)
    from_x = shift(far_sum, "xl", 1)
    second.add([far_sum])
    second.hop()
    right = second.add([])
    return finish(near, from_x, *right)


def solution(mesh):
    fine = Mesh(mesh.devices.reshape(8, 2, 2, 4, 2), ("z", "xl", "c", "y", "xh"))
    redist, summa = ("z", "xl", "c"), ("y", "xh")
    return jax.shard_map(
        per_device,
        mesh=fine,
        in_specs=(P(summa, redist), P(redist, summa)),
        out_specs=P(redist, summa),
        check_vma=False,
    )
```

```python
import functools

import jax
import jax.numpy as jnp
from jax import lax
from jax.experimental import pallas as pl
from jax.experimental.pallas import tpu as pltpu
from jax.sharding import Mesh, PartitionSpec as P

X_FIRST = 10
TILE = 256

SLOTS = 0x63745210

VMEM = pl.BlockSpec(memory_space=pltpu.VMEM)
SMEM = pl.BlockSpec(memory_space=pltpu.SMEM)
ANY = pl.BlockSpec(memory_space=pl.ANY)
HBM = pl.BlockSpec(memory_space=pltpu.HBM)

STEPS = ("zu", "zd", "x begin", "zu", "zd", "xu", "xd", "zu", "zd", "xu", "xd", "z end", "xu", "xd")

HEAVY, LIGHT = 20_000_000_000, 1


def shift(x, axis, by):
    n = lax.axis_size(axis)
    return lax.ppermute(x, axis, [(i, (i + by) % n) for i in range(n)])


def local(body, ins, deps, outs, scratch=(), scalars=(), through=(), pinned=True, big=(), weight=HEAVY, limit=4):
    pin = lambda x: pltpu.with_memory_space_constraint(x, pltpu.VMEM)
    sizes = [len(scalars), len(ins), len(big), len(through), len(deps), len(outs), len(through), len(scratch)]

    def kernel(*refs):
        groups, at = [], 0
        for n in sizes:
            groups.append(refs[at : at + n])
            at += n
        s, i, g, _, _, o, through_outs, t = groups
        body(*([s[0]] if s else []), [*i, *g], [*o, *through_outs], *([t] if t else []))

    kind = pltpu.VMEM if pinned else jax.ShapeDtypeStruct
    first = len(scalars) + len(ins) + len(big)
    return pl.pallas_call(
        kernel,
        in_specs=[SMEM] * len(scalars) + [VMEM] * len(ins) + [HBM] * len(big) + [VMEM] * len(through) + [ANY] * len(deps),
        out_specs=[VMEM] * (len(outs) + len(through)),
        out_shape=[kind(s, d) for s, d in outs] + [pltpu.VMEM(x.shape, x.dtype) for x in through],
        input_output_aliases={first + i: len(outs) + i for i in range(len(through))},
        scratch_shapes=list(scratch),
        compiler_params=pltpu.CompilerParams(vmem_limit_bytes=limit * 1024 * 1024),
        cost_estimate=pl.CostEstimate(flops=weight, bytes_accessed=1, transcendentals=0),
    )(*scalars, *map(pin, ins), *(pltpu.with_memory_space_constraint(x, pltpu.HBM) for x in big), *map(pin, through), *deps)


def split(x):
    high = x.astype(jnp.bfloat16)
    return high, (x - high.astype(jnp.float32)).astype(jnp.bfloat16)


def tile(i, first=0):
    return pl.ds(pl.multiple_of(first + i * TILE, 128), TILE)


def split_columns(b, sets, deps):
    depth, tiles = b.shape[0], b.shape[1] // TILE

    def body(ins, outs, scratch):
        held, sems = scratch

        def fetch(i):
            return pltpu.make_async_copy(ins[0].at[:, tile(i)], held.at[i], sems.at[i])

        for i in range(tiles):
            fetch(i).start()
        for j, (first, count) in enumerate(sets):

            @pl.loop(0, count)
            def _(i, j=j, first=first):
                fetch(first + i).wait()
                outs[2 * j][:, tile(i)], outs[2 * j + 1][:, tile(i)] = split(held[first + i])

    outs = [((depth, count * TILE), jnp.bfloat16) for _, count in sets for _ in range(2)]
    scratch = [pltpu.VMEM((tiles, depth, TILE), jnp.float32), pltpu.SemaphoreType.DMA((tiles,))]
    parts = local(body, [], deps, outs, scratch, big=[b], limit=12)
    return [parts[i : i + 2] for i in range(0, len(parts), 2)]


def products(panels, places, parts, deps, slots, into=(), joined=False, weight=HEAVY):
    count, depth = len(panels), parts[0][0].shape[0]
    mine = sorted({slot for *_, slot in places})
    first_slot, rows = mine[0], len(mine) * 64
    widths = [high.shape[1] for high, _ in parts]

    def body(ins, outs, scratch):
        a_high, a_low = scratch
        for ref, row, half, slot in places:
            to = half * rows + (slot - first_slot) * 64
            a_high[to : to + 64], a_low[to : to + 64] = split(ins[ref][row : row + 64])
        mul = functools.partial(jnp.dot, preferred_element_type=jnp.float32)
        block = slice(first_slot * 64, first_slot * 64 + rows)
        for j, width in enumerate(widths):
            high_ref, low_ref = ins[count + 2 * j : count + 2 * j + 2]
            keep_ref, send_ref = outs if joined else outs[2 * j : 2 * j + 2]
            first = sum(widths[:j]) if joined else 0
            for i in range(0, width, TILE):
                high, low = high_ref[:, i : i + TILE], low_ref[:, i : i + TILE]
                sums = mul(a_high[...], high) + (mul(a_low[...], high) + mul(a_high[...], low))
                keep_ref[block, first + i : first + i + TILE] = sums[:rows]
                send_ref[block, first + i : first + i + TILE] = sums[rows:]

    out_widths = [sum(widths)] if joined else widths
    outs = [] if into else [((slots * 64, width), jnp.float32) for width in out_widths for _ in range(2)]
    scratch = [pltpu.VMEM((2 * rows, depth), jnp.bfloat16)] * 2
    flat = [p for pair in parts for p in pair]
    return local(body, [*panels, *flat], deps, outs, scratch, through=into, weight=weight, limit=8)


def pack(up, down, other, deps):
    def body(ins, outs):
        up_ref, down_ref, other_ref = ins
        outs[0][:64], outs[0][64:] = other_ref[:64], up_ref[:64]
        outs[1][:64], outs[1][64:] = other_ref[64:], down_ref[64:]
        outs[2][:64], outs[2][64:] = up_ref[64:], down_ref[:64]

    return local(body, [up, down, other], deps, [(up.shape, jnp.float32)] * 3)


def late_halves(up, down, deps):
    def body(ins, outs):
        outs[0][...] = ins[0][:64]
        outs[1][...] = ins[1][:64]

    return local(body, [up, down], deps, [((64, up.shape[1]), jnp.float32)] * 2)


def x_part(lots, width, deps):
    def body(ins, outs):
        at = 0
        for kept, got, (_, _, col) in zip(ins[::2], ins[1::2], lots):
            for i in range(kept.shape[0] // 64):
                block = slice(64 * i + 32, 64 * i + 64), slice(col, col + width)
                outs[0][at : at + 32] = kept[block] + got[block]
                at += 32

    rows = sum(kept.shape[0] for kept, _, _ in lots) // 2
    return local(body, [v for lot in lots for v in lot[:2]], deps, [((rows, width), jnp.float32)], weight=LIGHT)[0]


def gate(deps):
    def body(ins, outs):
        outs[0][...] = jnp.zeros_like(outs[0])

    return local(body, [], deps, [((8, 128), jnp.float32)])


class Ring:
    def __init__(self, slots, lots, n, a, b, width):
        self.slots, self.lots, self.n, self.a, self.b, self.width = slots, lots, n, a, b, width

    def blocks(self, moves, outs, deps):
        n, width, arrays = self.n, self.width, []
        for _, lot in self.lots:
            arrays += [v for v, *_ in lot if not any(v is w for w in arrays)]
        where = lambda v: next(i for i, w in enumerate(arrays) if w is v)

        def body(slots, refs, out_refs):
            for out, at, k, low in moves:
                s = slots[k % 8]

                def write(first, lot):
                    starts = [pl.multiple_of((s - first) * stride + (row + low), n) for _, stride, row, _ in lot]

                    @pl.loop(0, width // TILE)
                    def _(i):
                        total = 0.0
                        for (v, _, _, col), start in zip(lot, starts):
                            total = total + refs[where(v)][pl.ds(start, n), tile(i, col)]
                        out_refs[out][at : at + n, tile(i)] = total

                for (first, end), lot in self.lots:
                    pl.when((s >= first) & (s < end))(functools.partial(write, first, lot))

        shapes = [((rows, width), jnp.float32) for rows in outs]
        return local(body, arrays, deps, shapes, scalars=[self.slots])

    def begin(self, deps):
        n, a, b = self.n, self.a, self.b
        moves = [(0, 0, 4, a), (0, n, 3, b), (1, 0, -4, b), (1, n, -3, a)]
        self.sends = list(self.blocks(moves, [2 * n, 2 * n], deps))
        return self.sends

    def hop(self, way):
        self.got[way].append(shift(self.sends[way], "z", 1 - 2 * way))

    def rest(self, deps):
        n, moves, rows = self.n, [], []
        for way, sign, long, short in ((0, 1, self.a, self.b), (1, -1, self.b, self.a)):
            for i in (3, 2, 1):
                moves.append((len(rows), 0, sign * i, long))
                if i > 1:
                    moves.append((len(rows), n, sign * (i - 1), short))
                rows.append(2 * n if i > 1 else n)
        moves += [(6, 0, 0, self.a), (7, 0, 0, self.b)]
        self.addends = self.blocks(moves, rows + [n, n], deps)
        self.got = [], []
        return self.addends[:1]

    def add(self, way, deps):
        got = self.got[way]
        addend = self.addends[3 * way + len(got) - 1]
        rows = addend.shape[0]

        def body(ins, outs):
            outs[0][...] = ins[0][:rows] + ins[1][...]

        self.sends[way] = local(body, [got[-1], addend], deps, [((rows, self.width), jnp.float32)])[0]
        return [self.sends[way]]

    def parts(self, which):
        return [self.addends[6 + which], self.got[which][3], self.got[1 - which][2]]


def add_up(terms, deps):
    n, width = terms[0].shape

    def body(ins, outs):
        outs[0][...] = ins[0][...] + ins[1][...] + ins[2][n:]

    return local(body, terms, deps, [((n, width), jnp.float32)])[0]


def finish(left, from_x, right_a, right_b):
    cut = from_x.shape[1]

    def body(ins, outs):
        total = lambda i: ins[i][...] + ins[i + 1][...] + ins[i + 2][ins[i].shape[0] :]
        outs[0][:, :cut] = 0.5 * (total(0) + ins[9][...])
        outs[0][:16, cut:] = 0.5 * total(3)
        outs[0][16:, cut:] = 0.5 * total(6)

    shape = (32, cut + right_a[0].shape[1])
    return local(body, [*left, *right_a, *right_b, from_x], [], [(shape, jnp.float32)], pinned=False)[0]


def per_device(amplitudes, integrals):
    z, xl, c = (lax.axis_index(n) for n in ("z", "xl", "c"))
    y, xh = lax.axis_index("y"), lax.axis_index("xh")
    depth, width = integrals.shape
    x_tiles = X_FIRST * 128 // TILE
    z_tiles = width // TILE - x_tiles

    owner = (z + jnp.arange(8, dtype=jnp.int32)) & 7
    code = (((owner >> 1) - y) & 3) * 2 + ((owner ^ xh) & 1)
    slots = (SLOTS >> (code * 4)) & 7

    own = amplitudes.reshape(2, 2, 32, depth)
    own = jnp.where(xl == 1, own[::-1], own)
    own = jnp.where(c == 1, own[:, ::-1], own)
    own = own.transpose(1, 0, 2, 3).reshape(128, depth)

    up, down, other = shift(own, "y", 1), shift(own, "y", -1), shift(own, "xh", 1)
    cut, x_width = z_tiles * TILE, x_tiles * TILE
    b_z, b_x = split_columns(integrals, ((0, z_tiles), (z_tiles, x_tiles)), [slots])
    both_halves = lambda ref, slot: [(ref, 64 * half, half, slot) for half in range(2)]
    own_blocks = products([own], both_halves(0, 0), [b_x, b_z], [], 4)
    packed_up, packed_down, packed_x = pack(up, down, other, [own_blocks[0]])
    up2, down2, other2 = shift(packed_up, "y", 1), shift(packed_down, "y", -1), shift(packed_x, "xh", 1)

    early_places = both_halves(0, 1) + both_halves(1, 2) + both_halves(2, 3)
    kept_x0, sent_x0, kept_z0, sent_z0 = products(
        [other, down, up], early_places, [b_x, b_z], [], 4, own_blocks, weight=LIGHT
    )
    got_x0, got_z0 = shift(sent_x0, "c", 1), shift(sent_z0, "c", 1)

    far_up, far_down = late_halves(up2, down2, [kept_z0, other2])
    other_far = [shift(far_up, "y", 1), shift(far_down, "y", -1)]
    x_send0 = x_part([(kept_x0, got_x0, 0)], x_width, [far_up])
    other0 = shift(x_send0, "xl", 1)

    late_places = [(0, 64, 0, 0), (1, 64, 1, 0), (2, 64, 0, 1), (1, 0, 1, 1), (0, 0, 0, 2), (2, 0, 1, 2)]
    kept1, sent1 = products([up2, down2, other2], late_places, [b_z, b_x], [x_send0], 3, joined=True)
    got1 = shift(sent1, "c", 1)
    kept_z2, sent_z2, kept_x2, sent_x2 = products(
        other_far, [(0, 0, 0, 0), (1, 0, 1, 0)], [b_z, b_x], [kept1, got_z0], 1
    )
    got_z2, got_x2 = shift(sent_z2, "c", 1), shift(sent_x2, "c", 1)

    z_lots = [
        ((0, 4), [(kept_z0, 64, 0, 0), (got_z0, 64, 0, 0)]),
        ((4, 7), [(kept1, 64, 0, 0), (got1, 64, 0, 0)]),
        ((7, 8), [(kept_z2, 64, 0, 0), (got_z2, 64, 0, 0)]),
    ]
    first = Ring(slots, z_lots, 32, 32, 0, cut)
    done = first.begin(gate([kept_z2]))
    done = first.rest(done)
    first.hop(0)
    first.hop(1)
    x_send1 = x_part([(kept1, got1, cut), (kept_x2, got_x2, 0)], x_width, [*done, other0])
    other1 = shift(x_send1, "xl", 1)
    x_lots = [
        ((0, 4), [(kept_x0, 64, 0, 0), (got_x0, 64, 0, 0), (other0, 32, 0, 0)]),
        ((4, 7), [(kept1, 64, 0, cut), (got1, 64, 0, cut), (other1, 32, 0, 0)]),
        ((7, 8), [(kept_x2, 64, 0, 0), (got_x2, 64, 0, 0), (other1, 32, 96, 0)]),
    ]
    second = Ring(slots, x_lots, 16, 0, 16, x_width)
    done = [x_send1]
    for step in STEPS:
        ring, way = (first, second)[step[0] == "x"], "ud".find(step[1])
        if step == "x begin":
            done = second.begin(done)
            done = second.rest(done)
            second.hop(0)
            second.hop(1)
        elif step == "z end":
            far_sum = add_up(first.parts(0), done)
            from_x = shift(far_sum, "xl", 1)
            done = [far_sum]
        else:
            done = ring.add(way, done)
            ring.hop(way)
    return finish(first.parts(1), from_x, second.parts(0), second.parts(1))


def solution(mesh):
    fine = Mesh(mesh.devices.reshape(8, 2, 2, 4, 2), ("z", "xl", "c", "y", "xh"))
    redist, summa = ("z", "xl", "c"), ("y", "xh")
    return jax.shard_map(
        per_device,
        mesh=fine,
        in_specs=(P(summa, redist), P(redist, summa)),
        out_specs=P(redist, summa),
        check_vma=False,
    )
```

```python
import functools

import jax
import jax.numpy as jnp
from jax import lax
from jax.experimental import pallas as pl
from jax.experimental.pallas import tpu as pltpu
from jax.sharding import Mesh, PartitionSpec as P

X_FIRST = 10
TILE = 256

SLOTS = 0x63745210

VMEM = pl.BlockSpec(memory_space=pltpu.VMEM)
SMEM = pl.BlockSpec(memory_space=pltpu.SMEM)
ANY = pl.BlockSpec(memory_space=pl.ANY)
HBM = pl.BlockSpec(memory_space=pltpu.HBM)

STEPS = ("zu", "zd", "x begin", "zu", "zd", "x rest", "xu", "xd", "zu", "zd", "xu", "xd", "z end", "xu", "xd")

HEAVY, LIGHT = 20_000_000_000, 1


def shift(x, axis, by):
    n = lax.axis_size(axis)
    return lax.ppermute(x, axis, [(i, (i + by) % n) for i in range(n)])


def local(body, ins, deps, outs, scratch=(), scalars=(), through=(), pinned=True, big=(), weight=HEAVY, limit=4):
    pin = lambda x: pltpu.with_memory_space_constraint(x, pltpu.VMEM)
    sizes = [len(scalars), len(ins), len(big), len(through), len(deps), len(outs), len(through), len(scratch)]

    def kernel(*refs):
        groups, at = [], 0
        for n in sizes:
            groups.append(refs[at : at + n])
            at += n
        s, i, g, _, _, o, through_outs, t = groups
        body(*([s[0]] if s else []), [*i, *g], [*o, *through_outs], *([t] if t else []))

    kind = pltpu.VMEM if pinned else jax.ShapeDtypeStruct
    first = len(scalars) + len(ins) + len(big)
    return pl.pallas_call(
        kernel,
        in_specs=[SMEM] * len(scalars) + [VMEM] * len(ins) + [HBM] * len(big) + [VMEM] * len(through) + [ANY] * len(deps),
        out_specs=[VMEM] * (len(outs) + len(through)),
        out_shape=[kind(s, d) for s, d in outs] + [pltpu.VMEM(x.shape, x.dtype) for x in through],
        input_output_aliases={first + i: len(outs) + i for i in range(len(through))},
        scratch_shapes=list(scratch),
        compiler_params=pltpu.CompilerParams(vmem_limit_bytes=limit * 1024 * 1024),
        cost_estimate=pl.CostEstimate(flops=weight, bytes_accessed=1, transcendentals=0),
    )(*scalars, *map(pin, ins), *(pltpu.with_memory_space_constraint(x, pltpu.HBM) for x in big), *map(pin, through), *deps)


def split(x):
    high = x.astype(jnp.bfloat16)
    return high, (x - high.astype(jnp.float32)).astype(jnp.bfloat16)


def tile(i, first=0):
    return pl.ds(pl.multiple_of(first + i * TILE, 128), TILE)


def split_columns(b, sets, deps):
    depth, tiles = b.shape[0], b.shape[1] // TILE

    def body(ins, outs, scratch):
        held, sems = scratch

        def fetch(i):
            return pltpu.make_async_copy(ins[0].at[:, tile(i)], held.at[i], sems.at[i])

        for i in range(tiles):
            fetch(i).start()
        for j, (first, count) in enumerate(sets):

            @pl.loop(0, count)
            def _(i, j=j, first=first):
                fetch(first + i).wait()
                outs[2 * j][:, tile(i)], outs[2 * j + 1][:, tile(i)] = split(held[first + i])

    outs = [((depth, count * TILE), jnp.bfloat16) for _, count in sets for _ in range(2)]
    scratch = [pltpu.VMEM((tiles, depth, TILE), jnp.float32), pltpu.SemaphoreType.DMA((tiles,))]
    parts = local(body, [], deps, outs, scratch, big=[b], limit=12)
    return [parts[i : i + 2] for i in range(0, len(parts), 2)]


def products(panels, places, parts, deps, slots, into=(), joined=False, weight=HEAVY):
    count, depth = len(panels), parts[0][0].shape[0]
    mine = sorted({slot for *_, slot in places})
    first_slot, rows = mine[0], len(mine) * 64
    widths = [high.shape[1] for high, _ in parts]

    def body(ins, outs, scratch):
        a_high, a_low = scratch
        for ref, row, half, slot in places:
            to = half * rows + (slot - first_slot) * 64
            a_high[to : to + 64], a_low[to : to + 64] = split(ins[ref][row : row + 64])
        mul = functools.partial(jnp.dot, preferred_element_type=jnp.float32)
        block = slice(first_slot * 64, first_slot * 64 + rows)
        for j, width in enumerate(widths):
            high_ref, low_ref = ins[count + 2 * j : count + 2 * j + 2]
            keep_ref, send_ref = outs if joined else outs[2 * j : 2 * j + 2]
            first = sum(widths[:j]) if joined else 0
            for i in range(0, width, TILE):
                high, low = high_ref[:, i : i + TILE], low_ref[:, i : i + TILE]
                sums = mul(a_high[...], high) + (mul(a_low[...], high) + mul(a_high[...], low))
                keep_ref[block, first + i : first + i + TILE] = sums[:rows]
                send_ref[block, first + i : first + i + TILE] = sums[rows:]

    out_widths = [sum(widths)] if joined else widths
    outs = [] if into else [((slots * 64, width), jnp.float32) for width in out_widths for _ in range(2)]
    scratch = [pltpu.VMEM((2 * rows, depth), jnp.bfloat16)] * 2
    flat = [p for pair in parts for p in pair]
    return local(body, [*panels, *flat], deps, outs, scratch, through=into, weight=weight, limit=8)


def pack(up, down, other, deps):
    def body(ins, outs):
        up_ref, down_ref, other_ref = ins
        outs[0][:64], outs[0][64:] = other_ref[:64], up_ref[:64]
        outs[1][:64], outs[1][64:] = other_ref[64:], down_ref[64:]
        outs[2][:64], outs[2][64:] = up_ref[64:], down_ref[:64]

    return local(body, [up, down, other], deps, [(up.shape, jnp.float32)] * 3)


def late_halves(up, down, deps):
    def body(ins, outs):
        outs[0][...] = ins[0][:64]
        outs[1][...] = ins[1][:64]

    return local(body, [up, down], deps, [((64, up.shape[1]), jnp.float32)] * 2, weight=LIGHT)


def x_part(lots, width, deps):
    def body(ins, outs):
        at = 0
        for kept, got, (_, _, col) in zip(ins[::2], ins[1::2], lots):
            for i in range(kept.shape[0] // 64):
                block = slice(64 * i + 32, 64 * i + 64), slice(col, col + width)
                outs[0][at : at + 32] = kept[block] + got[block]
                at += 32

    rows = sum(kept.shape[0] for kept, _, _ in lots) // 2
    return local(body, [v for lot in lots for v in lot[:2]], deps, [((rows, width), jnp.float32)], weight=LIGHT)[0]


def gate(deps):
    def body(ins, outs):
        outs[0][...] = jnp.zeros_like(outs[0])

    return local(body, [], deps, [((8, 128), jnp.float32)])


class Ring:
    def __init__(self, slots, lots, n, a, b, width):
        self.slots, self.lots, self.n, self.a, self.b, self.width = slots, lots, n, a, b, width

    def blocks(self, moves, outs, deps):
        n, width, arrays = self.n, self.width, []
        for _, lot in self.lots:
            arrays += [v for v, *_ in lot if not any(v is w for w in arrays)]
        where = lambda v: next(i for i, w in enumerate(arrays) if w is v)

        def body(slots, refs, out_refs):
            for out, at, k, low in moves:
                s = slots[k % 8]

                def write(first, lot):
                    starts = [pl.multiple_of((s - first) * stride + (row + low), n) for _, stride, row, _ in lot]

                    @pl.loop(0, width // TILE)
                    def _(i):
                        total = 0.0
                        for (v, _, _, col), start in zip(lot, starts):
                            total = total + refs[where(v)][pl.ds(start, n), tile(i, col)]
                        out_refs[out][at : at + n, tile(i)] = total

                for (first, end), lot in self.lots:
                    pl.when((s >= first) & (s < end))(functools.partial(write, first, lot))

        shapes = [((rows, width), jnp.float32) for rows in outs]
        return local(body, arrays, deps, shapes, scalars=[self.slots])

    def begin(self, deps):
        n, a, b = self.n, self.a, self.b
        moves = [(0, 0, 4, a), (0, n, 3, b), (1, 0, -4, b), (1, n, -3, a)]
        self.sends = list(self.blocks(moves, [2 * n, 2 * n], deps))
        self.got = [], []
        return self.sends

    def hop(self, way):
        pairs = [(2 * z + c, 2 * ((z + (1 - 2 * way) * (1 - 2 * c)) % 8) + c) for z in range(8) for c in range(2)]
        self.got[way].append(lax.ppermute(self.sends[way], ("z", "c"), pairs))

    def rest(self, deps):
        n, moves, rows = self.n, [], []
        for way, sign, long, short in ((0, 1, self.a, self.b), (1, -1, self.b, self.a)):
            for i in (3, 2, 1):
                moves.append((len(rows), 0, sign * i, long))
                if i > 1:
                    moves.append((len(rows), n, sign * (i - 1), short))
                rows.append(2 * n if i > 1 else n)
        moves += [(6, 0, 0, self.a), (7, 0, 0, self.b)]
        self.addends = self.blocks(moves, rows + [n, n], deps)
        return self.addends[:1]

    def add(self, way, deps):
        got = self.got[way]
        addend = self.addends[3 * way + len(got) - 1]
        rows = addend.shape[0]

        def body(ins, outs):
            outs[0][...] = ins[0][:rows] + ins[1][...]

        self.sends[way] = local(body, [got[-1], addend], deps, [((rows, self.width), jnp.float32)])[0]
        return [self.sends[way]]

    def parts(self, which):
        return [self.addends[6 + which], self.got[which][3], self.got[1 - which][2]]


def add_up(terms, deps):
    n, width = terms[0].shape

    def body(ins, outs):
        outs[0][...] = ins[0][...] + ins[1][...] + ins[2][n:]

    return local(body, terms, deps, [((n, width), jnp.float32)])[0]


def finish(left, from_x, right_a, right_b):
    cut = from_x.shape[1]

    def body(ins, outs):
        total = lambda i: ins[i][...] + ins[i + 1][...] + ins[i + 2][ins[i].shape[0] :]
        outs[0][:, :cut] = 0.5 * (total(0) + ins[9][...])
        outs[0][:16, cut:] = 0.5 * total(3)
        outs[0][16:, cut:] = 0.5 * total(6)

    shape = (32, cut + right_a[0].shape[1])
    return local(body, [*left, *right_a, *right_b, from_x], [], [(shape, jnp.float32)], pinned=False)[0]


def per_device(amplitudes, integrals):
    z, xl, c = (lax.axis_index(n) for n in ("z", "xl", "c"))
    y, xh = lax.axis_index("y"), lax.axis_index("xh")
    depth, width = integrals.shape
    x_tiles = X_FIRST * 128 // TILE
    z_tiles = width // TILE - x_tiles

    owner = (z + (1 - 2 * c) * jnp.arange(8, dtype=jnp.int32)) & 7
    code = (((owner >> 1) - y) & 3) * 2 + ((owner ^ xh) & 1)
    slots = (SLOTS >> (code * 4)) & 7

    own = amplitudes.reshape(2, 2, 32, depth)
    own = jnp.where(xl == 1, own[::-1], own)
    own = jnp.where(c == 1, own[:, ::-1], own)
    own = own.transpose(1, 0, 2, 3).reshape(128, depth)

    up, down, other = shift(own, "y", 1), shift(own, "y", -1), shift(own, "xh", 1)
    cut, x_width = z_tiles * TILE, x_tiles * TILE
    b_z, b_x = split_columns(integrals, ((0, z_tiles), (z_tiles, x_tiles)), [slots])
    both_halves = lambda ref, slot: [(ref, 64 * half, half, slot) for half in range(2)]
    own_blocks = products([own], both_halves(0, 0), [b_x, b_z], [], 4)
    packed_up, packed_down, packed_x = pack(up, down, other, [own_blocks[0]])
    up2, down2, other2 = shift(packed_up, "y", 1), shift(packed_down, "y", -1), shift(packed_x, "xh", 1)

    early_places = both_halves(0, 1) + both_halves(1, 2) + both_halves(2, 3)
    kept_x0, sent_x0, kept_z0, sent_z0 = products(
        [other, down, up], early_places, [b_x, b_z], [], 4, own_blocks, weight=LIGHT
    )
    got_x0, got_z0 = shift(sent_x0, "c", 1), shift(sent_z0, "c", 1)

    x_send0 = x_part([(kept_x0, got_x0, 0)], x_width, gate([kept_z0, up2, down2, other2]))
    other0 = shift(x_send0, "xl", 1)
    far_up, far_down = late_halves(up2, down2, [x_send0])
    other_far = [shift(far_up, "y", 1), shift(far_down, "y", -1)]

    late_places = [(0, 64, 0, 0), (1, 64, 1, 0), (2, 64, 0, 1), (1, 0, 1, 1), (0, 0, 0, 2), (2, 0, 1, 2)]
    kept1, sent1 = products([up2, down2, other2], late_places, [b_z, b_x], [far_up], 3, joined=True)
    got1 = shift(sent1, "c", 1)
    kept_z2, sent_z2, kept_x2, sent_x2 = products(
        other_far, [(0, 0, 0, 0), (1, 0, 1, 0)], [b_z, b_x], [kept1, got_z0], 1
    )
    got_z2, got_x2 = shift(sent_z2, "c", 1), shift(sent_x2, "c", 1)

    z_lots = [
        ((0, 4), [(kept_z0, 64, 0, 0), (got_z0, 64, 0, 0)]),
        ((4, 7), [(kept1, 64, 0, 0), (got1, 64, 0, 0)]),
        ((7, 8), [(kept_z2, 64, 0, 0), (got_z2, 64, 0, 0)]),
    ]
    first = Ring(slots, z_lots, 32, 32, 0, cut)
    done = first.begin(gate([kept_z2]))
    first.hop(0)
    first.hop(1)
    x_send1 = x_part([(kept1, got1, cut), (kept_x2, got_x2, 0)], x_width, [*done, other0])
    other1 = shift(x_send1, "xl", 1)
    done = first.rest([x_send1])
    x_lots = [
        ((0, 4), [(kept_x0, 64, 0, 0), (got_x0, 64, 0, 0), (other0, 32, 0, 0)]),
        ((4, 7), [(kept1, 64, 0, cut), (got1, 64, 0, cut), (other1, 32, 0, 0)]),
        ((7, 8), [(kept_x2, 64, 0, 0), (got_x2, 64, 0, 0), (other1, 32, 96, 0)]),
    ]
    second = Ring(slots, x_lots, 16, 0, 16, x_width)
    for step in STEPS:
        ring, way = (first, second)[step[0] == "x"], "ud".find(step[1])
        if step == "x begin":
            done = second.begin(done)
            second.hop(0)
            second.hop(1)
        elif step == "x rest":
            done = second.rest(done)
        elif step == "z end":
            far_sum = add_up(first.parts(0), done)
            from_x = shift(far_sum, "xl", 1)
            done = [far_sum]
        else:
            done = ring.add(way, done)
            ring.hop(way)
    return finish(first.parts(1), from_x, second.parts(0), second.parts(1))


def solution(mesh):
    fine = Mesh(mesh.devices.reshape(8, 2, 2, 4, 2), ("z", "xl", "c", "y", "xh"))
    redist, summa = ("z", "xl", "c"), ("y", "xh")
    return jax.shard_map(
        per_device,
        mesh=fine,
        in_specs=(P(summa, redist), P(redist, summa)),
        out_specs=P(redist, summa),
        check_vma=False,
    )
```

```python
import functools

import jax
import jax.numpy as jnp
from jax import lax
from jax.experimental import pallas as pl
from jax.experimental.pallas import tpu as pltpu
from jax.sharding import Mesh, PartitionSpec as P

X_FIRST = 10
TILE = 256

SLOTS = 0x63745210

VMEM = pl.BlockSpec(memory_space=pltpu.VMEM)
SMEM = pl.BlockSpec(memory_space=pltpu.SMEM)
ANY = pl.BlockSpec(memory_space=pl.ANY)
HBM = pl.BlockSpec(memory_space=pltpu.HBM)

STEPS = ("zu", "zd", "x begin", "zu", "zd", "x rest", "xu", "xd", "zu", "zd", "xu", "xd", "z end", "xu", "xd")

HEAVY, LIGHT = 20_000_000_000, 1


def shift(x, axis, by):
    n = lax.axis_size(axis)
    return lax.ppermute(x, axis, [(i, (i + by) % n) for i in range(n)])


def local(body, ins, deps, outs, scratch=(), scalars=(), through=(), pinned=True, big=(), weight=HEAVY, limit=4):
    pin = lambda x: pltpu.with_memory_space_constraint(x, pltpu.VMEM)
    sizes = [len(scalars), len(ins), len(big), len(through), len(deps), len(outs), len(through), len(scratch)]

    def kernel(*refs):
        groups, at = [], 0
        for n in sizes:
            groups.append(refs[at : at + n])
            at += n
        s, i, g, _, _, o, through_outs, t = groups
        body(*([s[0]] if s else []), [*i, *g], [*o, *through_outs], *([t] if t else []))

    kind = pltpu.VMEM if pinned else jax.ShapeDtypeStruct
    first = len(scalars) + len(ins) + len(big)
    return pl.pallas_call(
        kernel,
        in_specs=[SMEM] * len(scalars) + [VMEM] * len(ins) + [HBM] * len(big) + [VMEM] * len(through) + [ANY] * len(deps),
        out_specs=[VMEM] * (len(outs) + len(through)),
        out_shape=[kind(s, d) for s, d in outs] + [pltpu.VMEM(x.shape, x.dtype) for x in through],
        input_output_aliases={first + i: len(outs) + i for i in range(len(through))},
        scratch_shapes=list(scratch),
        compiler_params=pltpu.CompilerParams(vmem_limit_bytes=limit * 1024 * 1024),
        cost_estimate=pl.CostEstimate(flops=weight, bytes_accessed=1, transcendentals=0),
    )(*scalars, *map(pin, ins), *(pltpu.with_memory_space_constraint(x, pltpu.HBM) for x in big), *map(pin, through), *deps)


def split(x):
    high = x.astype(jnp.bfloat16)
    return high, (x - high.astype(jnp.float32)).astype(jnp.bfloat16)


def tile(i, first=0):
    return pl.ds(pl.multiple_of(first + i * TILE, 128), TILE)


def split_columns(b, sets, deps):
    depth, tiles = b.shape[0], b.shape[1] // TILE

    def body(ins, outs, scratch):
        held, sems = scratch

        def fetch(i):
            return pltpu.make_async_copy(ins[0].at[:, tile(i)], held.at[i], sems.at[i])

        for i in range(tiles):
            fetch(i).start()
        for j, (first, count) in enumerate(sets):

            @pl.loop(0, count)
            def _(i, j=j, first=first):
                fetch(first + i).wait()
                outs[2 * j][:, tile(i)], outs[2 * j + 1][:, tile(i)] = split(held[first + i])

    outs = [((depth, count * TILE), jnp.bfloat16) for _, count in sets for _ in range(2)]
    scratch = [pltpu.VMEM((tiles, depth, TILE), jnp.float32), pltpu.SemaphoreType.DMA((tiles,))]
    parts = local(body, [], deps, outs, scratch, big=[b], limit=12)
    return [parts[i : i + 2] for i in range(0, len(parts), 2)]


def products(panels, places, parts, deps, slots, into=(), joined=False, weight=HEAVY):
    count, depth = len(panels), parts[0][0].shape[0]
    mine = sorted({slot for *_, slot in places})
    first_slot, rows = mine[0], len(mine) * 64
    widths = [high.shape[1] for high, _ in parts]

    def body(ins, outs, scratch):
        a_high, a_low = scratch
        for ref, row, half, slot in places:
            to = half * rows + (slot - first_slot) * 64
            a_high[to : to + 64], a_low[to : to + 64] = split(ins[ref][row : row + 64])
        mul = functools.partial(jnp.dot, preferred_element_type=jnp.float32)
        block = slice(first_slot * 64, first_slot * 64 + rows)
        for j, width in enumerate(widths):
            high_ref, low_ref = ins[count + 2 * j : count + 2 * j + 2]
            keep_ref, send_ref = outs if joined else outs[2 * j : 2 * j + 2]
            first = sum(widths[:j]) if joined else 0
            for i in range(0, width, TILE):
                high, low = high_ref[:, i : i + TILE], low_ref[:, i : i + TILE]
                sums = mul(a_high[...], high) + (mul(a_low[...], high) + mul(a_high[...], low))
                keep_ref[block, first + i : first + i + TILE] = sums[:rows]
                send_ref[block, first + i : first + i + TILE] = sums[rows:]

    out_widths = [sum(widths)] if joined else widths
    outs = [] if into else [((slots * 64, width), jnp.float32) for width in out_widths for _ in range(2)]
    scratch = [pltpu.VMEM((2 * rows, depth), jnp.bfloat16)] * 2
    flat = [p for pair in parts for p in pair]
    return local(body, [*panels, *flat], deps, outs, scratch, through=into, weight=weight, limit=8)


def pack(up, down, other, deps):
    def body(ins, outs):
        up_ref, down_ref, other_ref = ins
        outs[0][:64], outs[0][64:] = other_ref[:64], up_ref[:64]
        outs[1][:64], outs[1][64:] = other_ref[64:], down_ref[64:]
        outs[2][:64], outs[2][64:] = up_ref[64:], down_ref[:64]

    return local(body, [up, down, other], deps, [(up.shape, jnp.float32)] * 3)


def late_halves(up, down, deps):
    def body(ins, outs):
        outs[0][...] = ins[0][:64]
        outs[1][...] = ins[1][:64]

    return local(body, [up, down], deps, [((64, up.shape[1]), jnp.float32)] * 2, weight=LIGHT)


def x_part(lots, width, deps):
    def body(ins, outs):
        at = 0
        for kept, got, (_, _, col) in zip(ins[::2], ins[1::2], lots):
            for i in range(kept.shape[0] // 64):
                block = slice(64 * i + 32, 64 * i + 64), slice(col, col + width)
                outs[0][at : at + 32] = kept[block] + got[block]
                at += 32

    rows = sum(kept.shape[0] for kept, _, _ in lots) // 2
    return local(body, [v for lot in lots for v in lot[:2]], deps, [((rows, width), jnp.float32)], weight=LIGHT)[0]


def gate(deps):
    def body(ins, outs):
        outs[0][...] = jnp.zeros_like(outs[0])

    return local(body, [], deps, [((8, 128), jnp.float32)])


class Ring:
    def __init__(self, slots, lots, n, a, b, width):
        self.slots, self.lots, self.n, self.a, self.b, self.width = slots, lots, n, a, b, width

    def blocks(self, moves, outs, deps):
        n, width, arrays = self.n, self.width, []
        for _, lot in self.lots:
            arrays += [v for v, *_ in lot if not any(v is w for w in arrays)]
        where = lambda v: next(i for i, w in enumerate(arrays) if w is v)

        def body(slots, refs, out_refs):
            for out, at, k, low in moves:
                s = slots[k % 8]

                def write(first, lot):
                    starts = [pl.multiple_of((s - first) * stride + (row + low), n) for _, stride, row, _ in lot]

                    @pl.loop(0, width // TILE)
                    def _(i):
                        total = 0.0
                        for (v, _, _, col), start in zip(lot, starts):
                            total = total + refs[where(v)][pl.ds(start, n), tile(i, col)]
                        out_refs[out][at : at + n, tile(i)] = total

                for (first, end), lot in self.lots:
                    pl.when((s >= first) & (s < end))(functools.partial(write, first, lot))

        shapes = [((rows, width), jnp.float32) for rows in outs]
        return local(body, arrays, deps, shapes, scalars=[self.slots])

    def begin(self, deps):
        n, a, b = self.n, self.a, self.b
        moves = [(0, 0, 4, a), (0, n, 3, b), (1, 0, -4, b), (1, n, -3, a)]
        self.sends = list(self.blocks(moves, [2 * n, 2 * n], deps))
        self.got = [], []
        return self.sends

    def hop(self, way):
        pairs = [(2 * z + c, 2 * ((z + (1 - 2 * way) * (1 - 2 * c)) % 8) + c) for z in range(8) for c in range(2)]
        self.got[way].append(lax.ppermute(self.sends[way], ("z", "c"), pairs))

    def rest(self, deps):
        n, moves, rows = self.n, [], []
        for way, sign, long, short in ((0, 1, self.a, self.b), (1, -1, self.b, self.a)):
            for i in (3, 2, 1):
                moves.append((len(rows), 0, sign * i, long))
                if i > 1:
                    moves.append((len(rows), n, sign * (i - 1), short))
                rows.append(2 * n if i > 1 else n)
        moves += [(6, 0, 0, self.a), (7, 0, 0, self.b)]
        self.addends = self.blocks(moves, rows + [n, n], deps)
        return self.addends[:1]

    def add(self, way, deps):
        got = self.got[way]
        addend = self.addends[3 * way + len(got) - 1]
        rows = addend.shape[0]

        def body(ins, outs):
            outs[0][...] = ins[0][:rows] + ins[1][...]

        self.sends[way] = local(body, [got[-1], addend], deps, [((rows, self.width), jnp.float32)])[0]
        return [self.sends[way]]

    def parts(self, which):
        return [self.addends[6 + which], self.got[which][3], self.got[1 - which][2]]


def add_up(terms, deps):
    n, width = terms[0].shape

    def body(ins, outs):
        outs[0][...] = ins[0][...] + ins[1][...] + ins[2][n:]

    return local(body, terms, deps, [((n, width), jnp.float32)])[0]


def finish(left, from_x, right_a, right_b, deps):
    cut = from_x.shape[1]

    def body(ins, outs):
        total = lambda i: ins[i][...] + ins[i + 1][...] + ins[i + 2][ins[i].shape[0] :]
        outs[0][:, :cut] = 0.5 * (total(0) + ins[9][...])
        outs[0][:16, cut:] = 0.5 * total(3)
        outs[0][16:, cut:] = 0.5 * total(6)

    shape = (32, cut + right_a[0].shape[1])
    return local(body, [*left, *right_a, *right_b, from_x], deps, [(shape, jnp.float32)], pinned=False)[0]


def per_device(amplitudes, integrals):
    z, xl, c = (lax.axis_index(n) for n in ("z", "xl", "c"))
    y, xh = lax.axis_index("y"), lax.axis_index("xh")
    depth, width = integrals.shape
    x_tiles = X_FIRST * 128 // TILE
    z_tiles = width // TILE - x_tiles

    owner = (z + (1 - 2 * c) * jnp.arange(8, dtype=jnp.int32)) & 7
    code = (((owner >> 1) - y) & 3) * 2 + ((owner ^ xh) & 1)
    slots = (SLOTS >> (code * 4)) & 7

    own = amplitudes.reshape(2, 2, 32, depth)
    own = jnp.where(xl == 1, own[::-1], own)
    own = jnp.where(c == 1, own[:, ::-1], own)
    own = own.transpose(1, 0, 2, 3).reshape(128, depth)

    up, down, other = shift(own, "y", 1), shift(own, "y", -1), shift(own, "xh", 1)
    cut, x_width = z_tiles * TILE, x_tiles * TILE
    b_z, b_x = split_columns(integrals, ((0, z_tiles), (z_tiles, x_tiles)), [slots])
    both_halves = lambda ref, slot: [(ref, 64 * half, half, slot) for half in range(2)]
    own_blocks = products([own], both_halves(0, 0), [b_x, b_z], [], 4)
    packed_up, packed_down, packed_x = pack(up, down, other, [own_blocks[0]])
    up2, down2, other2 = shift(packed_up, "y", 1), shift(packed_down, "y", -1), shift(packed_x, "xh", 1)

    early_places = both_halves(0, 1) + both_halves(1, 2) + both_halves(2, 3)
    kept_x0, sent_x0, kept_z0, sent_z0 = products(
        [other, down, up], early_places, [b_x, b_z], [], 4, own_blocks, weight=LIGHT
    )
    got_x0, got_z0 = shift(sent_x0, "c", 1), shift(sent_z0, "c", 1)

    x_send0 = x_part([(kept_x0, got_x0, 0)], x_width, gate([kept_z0, up2, down2, other2]))
    other0 = shift(x_send0, "xl", 1)
    far_up, far_down = late_halves(up2, down2, [x_send0])
    other_far = [shift(far_up, "y", 1), shift(far_down, "y", -1)]

    late_places = [(0, 64, 0, 0), (1, 64, 1, 0), (2, 64, 0, 1), (1, 0, 1, 1), (0, 0, 0, 2), (2, 0, 1, 2)]
    kept1, sent1 = products([up2, down2, other2], late_places, [b_z, b_x], [far_up], 3, joined=True)
    got1 = shift(sent1, "c", 1)
    kept_z2, sent_z2, kept_x2, sent_x2 = products(
        other_far, [(0, 0, 0, 0), (1, 0, 1, 0)], [b_z, b_x], [kept1, got_z0], 1
    )
    got_z2, got_x2 = shift(sent_z2, "c", 1), shift(sent_x2, "c", 1)

    z_lots = [
        ((0, 4), [(kept_z0, 64, 0, 0), (got_z0, 64, 0, 0)]),
        ((4, 7), [(kept1, 64, 0, 0), (got1, 64, 0, 0)]),
        ((7, 8), [(kept_z2, 64, 0, 0), (got_z2, 64, 0, 0)]),
    ]
    first = Ring(slots, z_lots, 32, 32, 0, cut)
    done = first.begin(gate([kept_z2]))
    first.hop(0)
    first.hop(1)
    x_send1 = x_part([(kept1, got1, cut), (kept_x2, got_x2, 0)], x_width, [*done, other0])
    other1 = shift(x_send1, "xl", 1)
    done = first.rest([x_send1])
    x_lots = [
        ((0, 4), [(kept_x0, 64, 0, 0), (got_x0, 64, 0, 0), (other0, 32, 0, 0)]),
        ((4, 7), [(kept1, 64, 0, cut), (got1, 64, 0, cut), (other1, 32, 0, 0)]),
        ((7, 8), [(kept_x2, 64, 0, 0), (got_x2, 64, 0, 0), (other1, 32, 96, 0)]),
    ]
    second = Ring(slots, x_lots, 16, 0, 16, x_width)
    for step in STEPS:
        ring, way = (first, second)[step[0] == "x"], "ud".find(step[1])
        if step == "x begin":
            done = second.begin(done)
            second.hop(0)
            second.hop(1)
        elif step == "x rest":
            done = second.rest(done)
        elif step == "z end":
            far_sum = add_up(first.parts(0), done)
            from_x = shift(far_sum, "xl", 1)
            done = [far_sum]
        else:
            done = ring.add(way, done)
            ring.hop(way)
    return finish(first.parts(1), from_x, second.parts(0), second.parts(1), gate(done))


def solution(mesh):
    fine = Mesh(mesh.devices.reshape(8, 2, 2, 4, 2), ("z", "xl", "c", "y", "xh"))
    redist, summa = ("z", "xl", "c"), ("y", "xh")
    return jax.shard_map(
        per_device,
        mesh=fine,
        in_specs=(P(summa, redist), P(redist, summa)),
        out_specs=P(redist, summa),
        check_vma=False,
    )
```

```python
import functools

import jax
import jax.numpy as jnp
from jax import lax
from jax.experimental import pallas as pl
from jax.experimental.pallas import tpu as pltpu
from jax.sharding import Mesh, PartitionSpec as P

X_FIRST = 10
TILE = 256

SLOTS = 0x63745210

VMEM = pl.BlockSpec(memory_space=pltpu.VMEM)
SMEM = pl.BlockSpec(memory_space=pltpu.SMEM)
ANY = pl.BlockSpec(memory_space=pl.ANY)
HBM = pl.BlockSpec(memory_space=pltpu.HBM)

STEPS = ("zu", "zd", "x begin", "zu", "zd", "x rest", "xu", "xd", "zu", "zd", "xu", "xd", "z end", "xu", "xd")

HEAVY, LIGHT = 20_000_000_000, 1


def shift(x, axis, by):
    n = lax.axis_size(axis)
    return lax.ppermute(x, axis, [(i, (i + by) % n) for i in range(n)])


def local(body, ins, deps, outs, scratch=(), scalars=(), through=(), pinned=True, big=(), weight=HEAVY, limit=4):
    pin = lambda x: pltpu.with_memory_space_constraint(x, pltpu.VMEM)
    sizes = [len(scalars), len(ins), len(big), len(through), len(deps), len(outs), len(through), len(scratch)]

    def kernel(*refs):
        groups, at = [], 0
        for n in sizes:
            groups.append(refs[at : at + n])
            at += n
        s, i, g, _, _, o, through_outs, t = groups
        body(*([s[0]] if s else []), [*i, *g], [*o, *through_outs], *([t] if t else []))

    kind = pltpu.VMEM if pinned else jax.ShapeDtypeStruct
    first = len(scalars) + len(ins) + len(big)
    return pl.pallas_call(
        kernel,
        in_specs=[SMEM] * len(scalars) + [VMEM] * len(ins) + [HBM] * len(big) + [VMEM] * len(through) + [ANY] * len(deps),
        out_specs=[VMEM] * (len(outs) + len(through)),
        out_shape=[kind(s, d) for s, d in outs] + [pltpu.VMEM(x.shape, x.dtype) for x in through],
        input_output_aliases={first + i: len(outs) + i for i in range(len(through))},
        scratch_shapes=list(scratch),
        compiler_params=pltpu.CompilerParams(vmem_limit_bytes=limit * 1024 * 1024),
        cost_estimate=pl.CostEstimate(flops=weight, bytes_accessed=1, transcendentals=0),
    )(*scalars, *map(pin, ins), *(pltpu.with_memory_space_constraint(x, pltpu.HBM) for x in big), *map(pin, through), *deps)


def split(x):
    high = x.astype(jnp.bfloat16)
    return high, (x - high.astype(jnp.float32)).astype(jnp.bfloat16)


def tile(i, first=0, size=TILE):
    return pl.ds(pl.multiple_of(first + i * size, 128), size)


def split_columns(b, sets, deps):
    depth, tiles = b.shape[0], b.shape[1] // TILE

    def body(ins, outs, scratch):
        held, sems = scratch

        def fetch(i):
            return pltpu.make_async_copy(ins[0].at[:, tile(i)], held.at[i], sems.at[i])

        for i in range(tiles):
            fetch(i).start()
        for j, (first, count) in enumerate(sets):

            @pl.loop(0, count)
            def _(i, j=j, first=first):
                fetch(first + i).wait()
                outs[2 * j][:, tile(i)], outs[2 * j + 1][:, tile(i)] = split(held[first + i])

    outs = [((depth, count * TILE), jnp.bfloat16) for _, count in sets for _ in range(2)]
    scratch = [pltpu.VMEM((tiles, depth, TILE), jnp.float32), pltpu.SemaphoreType.DMA((tiles,))]
    parts = local(body, [], deps, outs, scratch, big=[b], limit=12)
    return [parts[i : i + 2] for i in range(0, len(parts), 2)]


def products(panels, places, parts, deps, slots, into=(), joined=False, weight=HEAVY):
    count, depth = len(panels), parts[0][0].shape[0]
    mine = sorted({slot for *_, slot in places})
    first_slot, rows = mine[0], len(mine) * 64
    widths = [high.shape[1] for high, _ in parts]

    def body(ins, outs, scratch):
        a_high, a_low = scratch
        for ref, row, half, slot in places:
            to = half * rows + (slot - first_slot) * 64
            a_high[to : to + 64], a_low[to : to + 64] = split(ins[ref][row : row + 64])
        mul = functools.partial(jnp.dot, preferred_element_type=jnp.float32)
        block = slice(first_slot * 64, first_slot * 64 + rows)
        for j, width in enumerate(widths):
            high_ref, low_ref = ins[count + 2 * j : count + 2 * j + 2]
            keep_ref, send_ref = outs if joined else outs[2 * j : 2 * j + 2]
            first = sum(widths[:j]) if joined else 0
            for i in range(0, width, TILE):
                high, low = high_ref[:, i : i + TILE], low_ref[:, i : i + TILE]
                sums = mul(a_high[...], high) + (mul(a_low[...], high) + mul(a_high[...], low))
                keep_ref[block, first + i : first + i + TILE] = sums[:rows]
                send_ref[block, first + i : first + i + TILE] = sums[rows:]

    out_widths = [sum(widths)] if joined else widths
    outs = [] if into else [((slots * 64, width), jnp.float32) for width in out_widths for _ in range(2)]
    scratch = [pltpu.VMEM((2 * rows, depth), jnp.bfloat16)] * 2
    flat = [p for pair in parts for p in pair]
    return local(body, [*panels, *flat], deps, outs, scratch, through=into, weight=weight, limit=8)


def pack(up, down, other, deps):
    def body(ins, outs):
        up_ref, down_ref, other_ref = ins
        outs[0][:64], outs[0][64:] = other_ref[:64], up_ref[:64]
        outs[1][:64], outs[1][64:] = other_ref[64:], down_ref[64:]
        outs[2][:64], outs[2][64:] = up_ref[64:], down_ref[:64]

    return local(body, [up, down, other], deps, [(up.shape, jnp.float32)] * 3)


def late_halves(up, down, deps):
    def body(ins, outs):
        outs[0][...] = ins[0][:64]
        outs[1][...] = ins[1][:64]

    return local(body, [up, down], deps, [((64, up.shape[1]), jnp.float32)] * 2, weight=LIGHT)


def x_part(lots, width, deps):
    def body(ins, outs):
        at = 0
        for kept, got, (_, _, col) in zip(ins[::2], ins[1::2], lots):
            for i in range(kept.shape[0] // 64):
                block = slice(64 * i + 32, 64 * i + 64), slice(col, col + width)
                outs[0][at : at + 32] = kept[block] + got[block]
                at += 32

    rows = sum(kept.shape[0] for kept, _, _ in lots) // 2
    return local(body, [v for lot in lots for v in lot[:2]], deps, [((rows, width), jnp.float32)], weight=LIGHT)[0]


def gate(deps):
    def body(ins, outs):
        outs[0][...] = jnp.zeros_like(outs[0])

    return local(body, [], deps, [((8, 128), jnp.float32)])


class Ring:
    def __init__(self, slots, lots, n, a, b, width):
        self.slots, self.lots, self.n, self.a, self.b, self.width = slots, lots, n, a, b, width

    def blocks(self, moves, outs, deps):
        n, width, arrays = self.n, self.width, []
        for _, lot in self.lots:
            arrays += [v for v, *_ in lot if not any(v is w for w in arrays)]
        where = lambda v: next(i for i, w in enumerate(arrays) if w is v)

        def body(slots, refs, out_refs):
            for out, at, k, low in moves:
                s = slots[k % 8]

                def write(first, lot):
                    starts = [pl.multiple_of((s - first) * stride + (row + low), n) for _, stride, row, _ in lot]

                    @pl.loop(0, 2)
                    def _(i):
                        total = 0.0
                        for (v, _, _, col), start in zip(lot, starts):
                            total = total + refs[where(v)][pl.ds(start, n), tile(i, col, width // 2)]
                        out_refs[out][at : at + n, tile(i, 0, width // 2)] = total

                for (first, end), lot in self.lots:
                    pl.when((s >= first) & (s < end))(functools.partial(write, first, lot))

        shapes = [((rows, width), jnp.float32) for rows in outs]
        return local(body, arrays, deps, shapes, scalars=[self.slots])

    def begin(self, deps):
        n, a, b = self.n, self.a, self.b
        moves = [(0, 0, 4, a), (0, n, 3, b), (1, 0, -4, b), (1, n, -3, a)]
        self.sends = list(self.blocks(moves, [2 * n, 2 * n], deps))
        self.got = [], []
        return self.sends

    def hop(self, way):
        pairs = [(2 * z + c, 2 * ((z + (1 - 2 * way) * (1 - 2 * c)) % 8) + c) for z in range(8) for c in range(2)]
        self.got[way].append(lax.ppermute(self.sends[way], ("z", "c"), pairs))

    def rest(self, deps):
        n, moves, rows = self.n, [], []
        for way, sign, long, short in ((0, 1, self.a, self.b), (1, -1, self.b, self.a)):
            for i in (3, 2, 1):
                moves.append((len(rows), 0, sign * i, long))
                if i > 1:
                    moves.append((len(rows), n, sign * (i - 1), short))
                rows.append(2 * n if i > 1 else n)
        moves += [(6, 0, 0, self.a), (7, 0, 0, self.b)]
        self.addends = self.blocks(moves, rows + [n, n], deps)
        return self.addends[:1]

    def add(self, way, deps):
        got = self.got[way]
        addend = self.addends[3 * way + len(got) - 1]
        rows = addend.shape[0]

        def body(ins, outs):
            outs[0][...] = ins[0][:rows] + ins[1][...]

        self.sends[way] = local(body, [got[-1], addend], deps, [((rows, self.width), jnp.float32)])[0]
        return [self.sends[way]]

    def parts(self, which):
        return [self.addends[6 + which], self.got[which][3], self.got[1 - which][2]]


def add_up(terms, deps):
    n, width = terms[0].shape

    def body(ins, outs):
        outs[0][...] = ins[0][...] + ins[1][...] + ins[2][n:]

    return local(body, terms, deps, [((n, width), jnp.float32)])[0]


def finish(left, from_x, right_a, right_b, deps):
    cut = from_x.shape[1]

    def body(ins, outs):
        total = lambda i: ins[i][...] + ins[i + 1][...] + ins[i + 2][ins[i].shape[0] :]
        outs[0][:, :cut] = 0.5 * (total(0) + ins[9][...])
        outs[0][:16, cut:] = 0.5 * total(3)
        outs[0][16:, cut:] = 0.5 * total(6)

    shape = (32, cut + right_a[0].shape[1])
    return local(body, [*left, *right_a, *right_b, from_x], deps, [(shape, jnp.float32)], pinned=False)[0]


def per_device(amplitudes, integrals):
    z, xl, c = (lax.axis_index(n) for n in ("z", "xl", "c"))
    y, xh = lax.axis_index("y"), lax.axis_index("xh")
    depth, width = integrals.shape
    x_tiles = X_FIRST * 128 // TILE
    z_tiles = width // TILE - x_tiles

    owner = (z + (1 - 2 * c) * jnp.arange(8, dtype=jnp.int32)) & 7
    code = (((owner >> 1) - y) & 3) * 2 + ((owner ^ xh) & 1)
    slots = (SLOTS >> (code * 4)) & 7

    own = amplitudes.reshape(2, 2, 32, depth)
    own = jnp.where(xl == 1, own[::-1], own)
    own = jnp.where(c == 1, own[:, ::-1], own)
    own = own.transpose(1, 0, 2, 3).reshape(128, depth)

    up, down, other = shift(own, "y", 1), shift(own, "y", -1), shift(own, "xh", 1)
    cut, x_width = z_tiles * TILE, x_tiles * TILE
    b_z, b_x = split_columns(integrals, ((0, z_tiles), (z_tiles, x_tiles)), [slots])
    both_halves = lambda ref, slot: [(ref, 64 * half, half, slot) for half in range(2)]
    own_blocks = products([own], both_halves(0, 0), [b_x, b_z], [], 4)
    packed_up, packed_down, packed_x = pack(up, down, other, [own_blocks[0]])
    up2, down2, other2 = shift(packed_up, "y", 1), shift(packed_down, "y", -1), shift(packed_x, "xh", 1)

    early_places = both_halves(0, 1) + both_halves(1, 2) + both_halves(2, 3)
    kept_x0, sent_x0, kept_z0, sent_z0 = products(
        [other, down, up], early_places, [b_x, b_z], [], 4, own_blocks, weight=LIGHT
    )
    got_x0, got_z0 = shift(sent_x0, "c", 1), shift(sent_z0, "c", 1)

    x_send0 = x_part([(kept_x0, got_x0, 0)], x_width, gate([kept_z0, up2, down2, other2]))
    other0 = shift(x_send0, "xl", 1)
    far_up, far_down = late_halves(up2, down2, [x_send0])
    other_far = [shift(far_up, "y", 1), shift(far_down, "y", -1)]

    late_places = [(0, 64, 0, 0), (1, 64, 1, 0), (2, 64, 0, 1), (1, 0, 1, 1), (0, 0, 0, 2), (2, 0, 1, 2)]
    kept1, sent1 = products([up2, down2, other2], late_places, [b_z, b_x], [far_up], 3, joined=True)
    got1 = shift(sent1, "c", 1)
    kept_z2, sent_z2, kept_x2, sent_x2 = products(
        other_far, [(0, 0, 0, 0), (1, 0, 1, 0)], [b_z, b_x], [kept1, got_z0], 1
    )
    got_z2, got_x2 = shift(sent_z2, "c", 1), shift(sent_x2, "c", 1)

    z_lots = [
        ((0, 4), [(kept_z0, 64, 0, 0), (got_z0, 64, 0, 0)]),
        ((4, 7), [(kept1, 64, 0, 0), (got1, 64, 0, 0)]),
        ((7, 8), [(kept_z2, 64, 0, 0), (got_z2, 64, 0, 0)]),
    ]
    first = Ring(slots, z_lots, 32, 32, 0, cut)
    done = first.begin(gate([kept_z2]))
    first.hop(0)
    first.hop(1)
    x_send1 = x_part([(kept1, got1, cut), (kept_x2, got_x2, 0)], x_width, [*done, other0])
    other1 = shift(x_send1, "xl", 1)
    done = first.rest([x_send1])
    x_lots = [
        ((0, 4), [(kept_x0, 64, 0, 0), (got_x0, 64, 0, 0), (other0, 32, 0, 0)]),
        ((4, 7), [(kept1, 64, 0, cut), (got1, 64, 0, cut), (other1, 32, 0, 0)]),
        ((7, 8), [(kept_x2, 64, 0, 0), (got_x2, 64, 0, 0), (other1, 32, 96, 0)]),
    ]
    second = Ring(slots, x_lots, 16, 0, 16, x_width)
    for step in STEPS:
        ring, way = (first, second)[step[0] == "x"], "ud".find(step[1])
        if step == "x begin":
            done = second.begin(done)
            second.hop(0)
            second.hop(1)
        elif step == "x rest":
            done = second.rest(done)
        elif step == "z end":
            far_sum = add_up(first.parts(0), done)
            from_x = shift(far_sum, "xl", 1)
            done = [far_sum]
        else:
            done = ring.add(way, done)
            ring.hop(way)
    return finish(first.parts(1), from_x, second.parts(0), second.parts(1), gate(done))


def solution(mesh):
    fine = Mesh(mesh.devices.reshape(8, 2, 2, 4, 2), ("z", "xl", "c", "y", "xh"))
    redist, summa = ("z", "xl", "c"), ("y", "xh")
    return jax.shard_map(
        per_device,
        mesh=fine,
        in_specs=(P(summa, redist), P(redist, summa)),
        out_specs=P(redist, summa),
        check_vma=False,
    )
```
